128 devices in a mesh: row: 16 (over y, z), col: 8 (over x, core).
Axes of the slice: x: 4, y: 4, z: 4, core: 2. Of those that a mesh axis runs over, the one named last changes fastest.
Arguments:
- solved: bfloat16 [8192, 16384], P('col', 'row'), may hold values from -6 to 6
- factor_rows: bfloat16 [1024, 8192], P(None, 'col'), may hold values from -0.0625 to 0.0625
- diag_inverse: bfloat16 [1024, 1024], replicated, may hold values from -1 to 1, as said below
- features: bfloat16 [16384, 1024], P('row'), may hold values from -6 to 6
- covariance: float32 [16384, 16384], P('row', 'col'), may hold values from -6 to 6
Outputs:
- cov_out: float32 [16384, 16384], P('row', 'col')
The draws below stay inside these ranges and needn't reach their ends.
Inputs may be any that keep to these rules, and one draw needn't show every extreme that they name: diag_inverse is lower triangular; its diagonal lies between 1 / sqrt(1024) and 3 / sqrt(1024).
All inputs are finite; a program needn't handle non-finite values.
Results may differ from the reference program's by a relative error of at most 0.0018.
Values may be sent and summed in bfloat16 or wider, within the bound.
A program may use at most 128 MiB of HBM per device.

```python
import jax
import jax.numpy as jnp
from jax import lax

B = 1024
K0 = 8192
N = 16384


def draw_diag_inverse(key, part):
    base = jax.random.fold_in(key, 7)
    first, second = jax.random.split(base)
    diagonal = jax.random.uniform(first, (B,), jnp.float32, 1.0, 3.0)
    lower = jax.random.normal(second, (B, B), jnp.float32) / jnp.sqrt(jnp.float32(B))
    matrix = jnp.tril(lower, -1) + jnp.diag(diagonal)
    return (matrix / jnp.sqrt(jnp.float32(B))).astype(jnp.bfloat16)


def level_of(key, dims, cuts, smallest, top_value):
    factor_of = 1.0
    for dim, parts in cuts:
        steps = jax.random.uniform(jax.random.fold_in(jax.random.fold_in(key, 6), dim), (parts,), jnp.float32, smallest / len(cuts), top_value / len(cuts))
        factor_of = factor_of * jnp.repeat(jnp.exp(steps), dims[dim] // parts).reshape((-1,) + (1,) * (len(dims) - 1 - dim))
    return factor_of


def scatter_about(key, dims, spread, bound, shards=(), kind=jnp.bfloat16):
    result = jax.random.normal(key, dims, jnp.float32) * spread
    if len(shards) > 0:
        result = level_of(key, dims, shards, -0.22, 0.18) * result
    return jnp.clip(result, min=-bound, max=bound).astype(kind)


def setup_inputs(seed: int = 0) -> dict:
    streams_of = jax.random.split(jax.random.key(seed), 6)
    return {
        "solved": scatter_about(streams_of[0], (K0, N), 1.0, 6.0, ((0, 8), (1, 16))),
        "factor_rows": scatter_about(streams_of[1], (B, K0), K0 ** -0.5, 0.0625, ((1, 8),)),
        "diag_inverse": draw_diag_inverse(jax.random.fold_in(streams_of[5], 71), 0),
        "features": scatter_about(streams_of[3], (N, B), 1.0, 6.0, ((0, 16),)),
        "covariance": scatter_about(streams_of[4], (N, N), 1.0, 6.0, ((0, 16), (1, 8)), jnp.float32),
    }


def reference(solved, factor_rows, diag_inverse, features, covariance):
    high = lax.Precision.HIGHEST
    summed = jnp.dot(solved.astype(jnp.float32).T, factor_rows.astype(jnp.float32).T, precision=high)
    residual = (features.astype(jnp.float32) - summed).astype(jnp.bfloat16)
    panel = jnp.dot(residual.astype(jnp.float32), diag_inverse.astype(jnp.float32).T, precision=high).astype(jnp.bfloat16)
    wide = panel.astype(jnp.float32)
    return covariance + jnp.dot(wide, wide.T, precision=high)
```

```python
import jax
import jax.numpy as jnp
from jax import lax
from jax.experimental import pallas as pl
from jax.experimental.pallas import tpu as pltpu
from jax.sharding import PartitionSpec as P

F32 = jnp.float32
BF16 = jnp.bfloat16
CHUNKS = 4
KB = 256
NT = (((1,), (1,)), ((), ()))

ORDERS = (13882568, 2178540, 6835325, 16075976, 10973347, 2185148, 2189180, 10973347, 14592200, 4579820, 5801852, 14592088, 16114952, 7052332, 8217132, 16373000)
LOW = (22442, 1536, 0, 128, 56512, 1088, 8192, 41472, 56366, 5126, 2, 36994, 2798, 117, 1, 34848)
HIGH = (8, 55267, 1808, 256, 32769, 55565, 278, 12288, 6192, 53412, 4100, 4128, 2817, 2156, 68, 48)


def pick(table, role):
    value = jnp.int32(table[0])
    for index in range(1, len(table)):
        value = jnp.where(role == index, jnp.int32(table[index]), value)
    return value


def kernel(
    solved, factor, dinv, features, covariance, acc,
    sv, fv, dv, fe, res, own, sib_out, sib_in, red_out, red_in, row_panel, col_panel,
    load_sem, sv_sem, sib_s, sib_r, red_s, red_r, gat_s, gat_r, tree_s, tree_r,
):
    row = lax.axis_index("row")
    col = lax.axis_index("col")
    y, z = row // 4, row % 4
    x, core = col // 2, col % 2

    def at(xx, yy, zz, cc):
        return {"row": ((yy + 4) % 4) * 4 + (zz + 4) % 4, "col": ((xx + 4) % 4) * 2 + cc}

    sibling = at(x, y, z, 1 - core)
    x_next, x_prev = at(x + 1, y, z, core), at(x - 1, y, z, core)
    around = (at(x, y + 1, z, core), at(x, y - 1, z, core), at(x, y, z + 1, core), at(x, y, z - 1, core))

    role = ((y - x + 4) % 4) * 4 + (z - 2 * core + 4) % 4
    order, low, high = pick(ORDERS, role), pick(LOW, role), pick(HIGH, role)
    is_source = role < 2

    def remote(src, dst, send, recv, device):
        return pltpu.make_async_remote_copy(
            src_ref=src, dst_ref=dst, send_sem=send, recv_sem=recv,
            device_id=device, device_id_type=pl.DeviceIdType.MESH,
        )

    def frames_of(place):
        chip = (x + place % 4) % 4
        half = core if place < 4 else 1 - core
        return pl.multiple_of(chip * 256 + half * 128, 128)

    def sv_load(place):
        return pltpu.make_async_copy(
            solved.at[:, pl.ds(frames_of(place), 128)], sv.at[:, pl.ds(place * 128, 128)], sv_sem.at[place]
        )

    fv_loads = [
        pltpu.make_async_copy(factor.at[pl.ds(k * KB, KB)], fv.at[pl.ds(k * KB, KB)], load_sem.at[k])
        for k in range(CHUNKS)
    ]
    fe_load = pltpu.make_async_copy(features.at[pl.ds(frames_of(0), 128)], fe, load_sem.at[4])
    dv_load = pltpu.make_async_copy(dinv, dv, load_sem.at[5])
    acc_load = pltpu.make_async_copy(covariance, acc, load_sem.at[6])

    fv_loads[0].start()
    for place in (4, 5, 6, 7, 0, 1, 2, 3):
        sv_load(place).start()
    for k in range(1, CHUNKS):
        fv_loads[k].start()
    fe_load.start()
    dv_load.start()
    acc_load.start()

    barrier = pltpu.get_barrier_semaphore()
    for device in (sibling, x_next, x_prev) + around:
        pl.semaphore_signal(barrier, inc=1, device_id=device, device_id_type=pl.DeviceIdType.MESH)

    def rows_of(k):
        return pl.ds(pl.multiple_of(k * KB, KB), KB)

    def sib_copy(k):
        return remote(sib_out.at[k], sib_in.at[k], sib_s.at[k], sib_r.at[k], sibling)

    def red_copy(k, m):
        return remote(
            red_out.at[k, m], red_in.at[k, m], red_s.at[k, m], red_r.at[k, m], x_next if m % 2 == 0 else x_prev
        )

    def partial_sibling(k):
        sib_out[k] = jnp.dot(fv[rows_of(k), :], sv[:, 512:], preferred_element_type=F32).astype(BF16)

    def partial_own(k):
        own[k] = jnp.dot(fv[rows_of(k), :], sv[:, :512], preferred_element_type=F32)

    def reduce_start(k):
        sib_copy(k).wait_recv()
        total = own[k] + sib_in[k].astype(F32)
        own[k] = total
        red_out[k, 0] = total[:128, 256:384].astype(BF16)
        red_out[k, 1] = total[128:, 256:384].astype(BF16)
        red_copy(k, 0).start()
        red_copy(k, 1).start()
        red_out[k, 2] = total[128:, 128:256].astype(BF16)
        red_out[k, 3] = total[:128, 384:].astype(BF16)
        red_copy(k, 2).start()
        red_copy(k, 3).start()

    def reduce_merge(k):
        red_copy(k, 0).wait_recv()
        red_out[k, 4] = (own[k, :128, 128:256] + red_in[k, 0].astype(F32)).astype(BF16)
        red_copy(k, 4).start()
        red_copy(k, 1).wait_recv()
        red_out[k, 5] = (own[k, 128:, 384:] + red_in[k, 1].astype(F32)).astype(BF16)
        red_copy(k, 5).start()

    def piece(k, chip, half, offset=0, size=128):
        first = pl.multiple_of(((chip + 4) % 4) * 256 + half * 128 + offset, 64)
        return row_panel.at[k, pl.ds(first, size)]

    def gather_copy(k, m):
        ref = (
            lambda: piece(k, x, core),
            lambda: piece(k, x, core),
            lambda: piece(k, x - 1, core, 0, 64),
            lambda: piece(k, x + 1, core, 64, 64),
            lambda: piece(k, x, core),
            lambda: piece(k, x - 1, core),
            lambda: piece(k, x + 1, core),
            lambda: piece(k, x + 2, core),
        )[m]()
        device = (x_next, x_prev, x_next, x_prev, sibling, sibling, sibling, sibling)[m]
        return remote(ref, ref, gat_s.at[k, m], gat_r.at[k, m], device)

    def unit(k, u):
        return col_panel.at[k, u]

    def own_unit(k, j):
        @pl.when(is_source)
        def _():
            first = pl.multiple_of(((x + j) % 4) * 256, 256)
            pltpu.make_async_copy(
                row_panel.at[k, pl.ds(first, 256)], unit(k, role * 4 + j), tree_r.at[k, role * 4 + j]
            ).start()

    def make_panel(k):
        for m in (2, 3, 4, 5):
            red_copy(k, m).wait_recv()
        top = own[k, :128, :128] + red_in[k, 4].astype(F32) + red_in[k, 3].astype(F32)
        bottom = own[k, 128:, :128] + red_in[k, 5].astype(F32) + red_in[k, 2].astype(F32)
        summed = jnp.concatenate([top.T, bottom.T], axis=1)
        cols = pl.ds(pl.multiple_of(k * KB, KB), KB)
        res[:, cols] = (fe[:, cols].astype(F32) - summed).astype(BF16)
        panel = lax.dot_general(res[...], dv[rows_of(k), :], NT, preferred_element_type=F32).astype(BF16)
        first = pl.multiple_of(x * 256 + core * 128, 128)
        row_panel[k, pl.ds(first, 128)] = panel
        gather_copy(k, 0).start()
        gather_copy(k, 1).start()
        gather_copy(k, 4).start()

    def gather_pass(k):
        gather_copy(k, 0).wait_recv()
        gather_copy(k, 2).start()
        gather_copy(k, 5).start()
        gather_copy(k, 1).wait_recv()
        gather_copy(k, 3).start()
        gather_copy(k, 6).start()
        gather_copy(k, 4).wait_recv()
        own_unit(k, 0)

    def gather_opposite(k):
        gather_copy(k, 2).wait_recv()
        gather_copy(k, 3).wait_recv()
        gather_copy(k, 7).start()
        gather_copy(k, 5).wait_recv()
        own_unit(k, 3)
        gather_copy(k, 6).wait_recv()
        own_unit(k, 1)

    def gather_end(k):
        gather_copy(k, 7).wait_recv()
        own_unit(k, 2)

    res[...] = jnp.zeros_like(res)
    fv_loads[0].wait()
    for place in (4, 5, 6, 7):
        sv_load(place).wait()
    partial_sibling(0)
    pl.semaphore_wait(barrier, 7)
    sib_copy(0).start()
    for place in (0, 1, 2, 3):
        sv_load(place).wait()
    partial_own(0)
    reduce_start(0)
    fv_loads[1].wait()
    partial_sibling(1)
    sib_copy(1).start()
    partial_own(1)
    reduce_merge(0)
    fv_loads[2].wait()
    partial_sibling(2)
    sib_copy(2).start()
    partial_own(2)
    fe_load.wait()
    dv_load.wait()
    make_panel(0)
    reduce_start(1)
    fv_loads[3].wait()
    partial_sibling(3)
    sib_copy(3).start()
    gather_pass(0)
    partial_own(3)
    reduce_merge(1)
    gather_opposite(0)
    gather_end(0)
    acc_load.wait()

    def tree_copy(k, u, d):
        return remote(unit(k, u), unit(k, u), tree_s.at[k, u, d], tree_r.at[k, u], around[d])

    def passes(u, d):
        word = jnp.where(u < 4, low, high)
        place = (u % 4) * 4 + d
        return (lax.shift_right_logical(word, place) & 1) == 1

    @pl.loop(0, CHUNKS * 8)
    def _(t):
        k, i = t // 8, t % 8
        for stage, when, ahead in (
            (make_panel, 0, 1), (reduce_start, 1, 2), (gather_pass, 2, 1), (reduce_merge, 3, 2),
            (gather_opposite, 5, 1), (gather_end, 7, 1),
        ):
            @pl.when(jnp.logical_and(i == when, k + ahead < CHUNKS))
            def _():
                stage(k + ahead)

        u = lax.shift_right_logical(order, 3 * i) & 7
        tree_copy(k, u, 0).wait_recv()
        for d in range(4):
            @pl.when(passes(u, d))
            def _():
                tree_copy(k, u, d).start()
        first = pl.multiple_of((u // 4) * 1024 + ((x + u % 4) % 4) * 256, 256)
        acc[:, pl.ds(first, 256)] += lax.dot_general(
            row_panel[k], col_panel[k, u], NT, preferred_element_type=F32
        )

    @pl.loop(0, CHUNKS * 8)
    def _(t):
        k, u = t // 8, t % 8
        for d in range(4):
            @pl.when(passes(u, d))
            def _():
                tree_copy(k, u, d).wait_send()

    @pl.loop(0, CHUNKS)
    def _(k):
        sib_copy(k).wait_send()
        for m in range(6):
            red_copy(k, m).wait_send()
        for m in range(8):
            gather_copy(k, m).wait_send()


def body(solved, factor_rows, diag_inverse, features, covariance):
    any_place = pl.BlockSpec(memory_space=pl.ANY)
    dma = pltpu.SemaphoreType.DMA
    return pl.pallas_call(
        kernel,
        out_shape=pltpu.VMEM((1024, 2048), F32),
        in_specs=[any_place] * 5,
        out_specs=pl.BlockSpec(memory_space=pltpu.VMEM),
        scratch_shapes=[
            pltpu.VMEM((1024, 1024), BF16),
            pltpu.VMEM((1024, 1024), BF16),
            pltpu.VMEM((1024, 1024), BF16),
            pltpu.VMEM((128, 1024), BF16),
            pltpu.VMEM((128, 1024), BF16),
            pltpu.VMEM((CHUNKS, KB, 512), F32),
            pltpu.VMEM((CHUNKS, KB, 512), BF16),
            pltpu.VMEM((CHUNKS, KB, 512), BF16),
            pltpu.VMEM((CHUNKS, 6, 128, 128), BF16),
            pltpu.VMEM((CHUNKS, 6, 128, 128), BF16),
            pltpu.VMEM((CHUNKS, 1024, KB), BF16),
            pltpu.VMEM((CHUNKS, 8, 256, KB), BF16),
            dma((7,)),
            dma((8,)),
            dma((CHUNKS,)),
            dma((CHUNKS,)),
            dma((CHUNKS, 6)),
            dma((CHUNKS, 6)),
            dma((CHUNKS, 8)),
            dma((CHUNKS, 8)),
            dma((CHUNKS, 8, 4)),
            dma((CHUNKS, 8)),
        ],
        compiler_params=pltpu.CompilerParams(
            collective_id=0, has_side_effects=True, vmem_limit_bytes=44 * 2**20
        ),
        cost_estimate=pl.CostEstimate(flops=7 * 10**9, bytes_accessed=24 * 10**6, transcendentals=0),
    )(solved, factor_rows, diag_inverse, features, covariance)


def solution(mesh):
    placed = (P("col", "row"), P(None, "col"), P(), P("row", None), P("row", "col"))
    return jax.shard_map(
        body, mesh=mesh, in_specs=placed, out_specs=P("row", "col"), check_vma=False
    )
```

```python
import jax
import jax.numpy as jnp
from jax import lax
from jax.experimental import pallas as pl
from jax.experimental.pallas import tpu as pltpu
from jax.sharding import PartitionSpec as P

F32 = jnp.float32
BF16 = jnp.bfloat16
CHUNKS = 4
KB = 256
NT = (((1,), (1,)), ((), ()))
MESH = pl.DeviceIdType.MESH

(
    PART_SIBLING, PART_OWN, REDUCE, PANEL, FROM_PREV, FROM_NEXT, FROM_OPPOSITE, ROW_DONE,
) = range(8)
SOURCE, PASS, USE, NOTHING = 8, 12, 20, 31
LOW = (65510, 17936, 768, 0, 56448, 16576, 32, 258, 50190, 21507, 2, 138, 35562, 96, 1, 32808)
HIGH = (2056, 24555, 80, 8456, 45312, 55564, 84, 12352, 6272, 20652, 4613, 1, 0, 3178, 1600, 64)
STEPS = (
    (134254752, 205004962, 206102787, 83952264, 19063174, 78385680, 42222891, 46516932, 151407654, 89223593, 118348468, 114396434, 154412520, 120353508, 179939914, 221613459, 223751147, 247274802, 124582902, 187989104, 255618386, 192216434, 65535475, 65523615),
    (134254752, 205004962, 206102787, 83952264, 19063174, 78320140, 42108843, 52825028, 44258074, 208065736, 109748911, 30301239, 219063062, 210918859, 177383013, 225864806, 189617897, 114013531, 259964152, 183761516, 181643981, 251394797, 65534830, 65523615),
    (134254752, 205004962, 206102787, 13173380, 77914503, 80103579, 208591271, 145082308, 150048018, 213458097, 52004911, 117033484, 109780274, 117807118, 187985363, 190089869, 255622643, 169650764, 114015576, 181644239, 251394668, 249273005, 179534960, 65534701),
    (134254752, 205004962, 206102787, 13173380, 77848967, 80037527, 208013351, 145627204, 52714415, 46375878, 111899364, 114013158, 183749906, 185863571, 179522060, 124574897, 247163726, 251386412, 122469230, 253504721, 255617612, 192212306, 259849586, 65534572),
    (134254752, 205004962, 206102787, 140608132, 14930469, 50602647, 100194342, 118346692, 25398675, 92637766, 107819621, 97639910, 166103350, 44266455, 106146896, 236710714, 253618764, 52718062, 190102363, 111902195, 257735276, 179526833, 187988717, 65535217),
    (134254752, 205004962, 206102787, 140608132, 76288656, 145097619, 108581659, 124654532, 54823823, 210060998, 185869285, 105764838, 235243322, 251987559, 52719059, 190094126, 259845071, 111893036, 120356210, 179530574, 177421295, 249395053, 245050577, 65535217),
    (134254752, 205004962, 206102787, 13189637, 75768199, 82417688, 40989112, 52716059, 210559942, 214168251, 44256231, 185493553, 42146735, 109788272, 191211918, 54831311, 259845335, 255613613, 179526962, 233548364, 247167926, 190098254, 249281132, 65535346),
    (134254752, 205004962, 206102787, 13189637, 80290183, 32600487, 50602519, 118236102, 117010991, 216462099, 46466574, 124570769, 166402862, 102984628, 164895893, 54832214, 177421295, 175913838, 259849307, 187520721, 255614258, 179534444, 257731922, 65534701),
    (134254752, 205004962, 206102787, 140608132, 25285284, 92906004, 109699811, 50596751, 101009094, 99496676, 41526199, 159828750, 176583569, 124606893, 113674542, 245050319, 179530832, 120347954, 181648367, 253504979, 190102253, 259849070, 257731793, 65535217),
    (134254752, 205004962, 206102787, 140608132, 33673892, 101294616, 118088419, 42143123, 92693265, 107819748, 33137595, 216434967, 99879565, 122465335, 119899953, 253504076, 114011603, 183753389, 188426450, 255621722, 251395571, 164980466, 247168342, 65534830),
    (134254752, 205004962, 206102787, 13173380, 80306567, 34681255, 118235800, 213459910, 42143123, 52720614, 124590508, 54823823, 120343181, 116124752, 159620402, 253504022, 191715027, 190094126, 183758033, 238877292, 259964146, 250963695, 247163726, 65534830),
    (134254752, 205004962, 206102787, 13173380, 80306567, 26292647, 109781652, 213459910, 217680783, 100879376, 116120597, 177409427, 52710158, 54827693, 183754163, 114014828, 122465360, 120351437, 181648367, 190102640, 249394926, 187985363, 257736179, 65535217),
    (134254752, 205004962, 206102787, 140608005, 76223116, 145032079, 80087952, 208407181, 109699631, 46373943, 211379782, 177330861, 38639462, 245052314, 183757904, 40676045, 36936987, 247163673, 253500851, 173784047, 120355674, 192216434, 255618257, 65535475),
    (134254752, 205004962, 206102787, 140608005, 76288656, 144985095, 144233241, 54828071, 168117958, 120353381, 41528391, 26122523, 46379924, 96213548, 124582965, 48491729, 255618386, 179535218, 114006959, 247163468, 181644755, 245050319, 259849070, 65534959),
    (134254752, 205004962, 206102787, 13189637, 80290183, 143749543, 52758668, 150051372, 48493157, 50606866, 100889498, 120347669, 115788207, 177413426, 108288685, 190098619, 48002574, 185875700, 257731535, 114010829, 236714733, 192216183, 249277262, 65535475),
    (134254752, 205004962, 206102787, 13189637, 75702663, 82417172, 32600500, 44261911, 212591558, 214151735, 216418454, 111897164, 113674542, 50608748, 183392463, 179526704, 181640498, 247156115, 234118579, 232045529, 255621978, 257731664, 253163603, 65535475),
)


def pick(table, role):
    value = jnp.int32(table[0])
    for index in range(1, len(table)):
        value = jnp.where(role == index, jnp.int32(table[index]), value)
    return value


def kernel(
    solved, factor, dinv, features, covariance, acc,
    sv, fv, dv, fe, res, own, sib_out, sib_in, red_out, red_in, panels,
    load_sem, sv_sem, sib_s, sib_r, red_s, red_r, gat_s, gat_r, tree_s, tree_r,
):
    row = lax.axis_index("row")
    col = lax.axis_index("col")
    y, z = row // 4, row % 4
    x, core = col // 2, col % 2

    def at(xx, yy, zz, cc):
        return {"row": ((yy + 4) % 4) * 4 + (zz + 4) % 4, "col": ((xx + 4) % 4) * 2 + cc}

    sibling = at(x, y, z, 1 - core)
    along = (at(x + 1, y, z, core), at(x - 1, y, z, core), at(x + 2, y, z, core))
    around = (at(x, y + 1, z, core), at(x, y - 1, z, core), at(x, y, z + 1, core), at(x, y, z - 1, core))

    role = ((y - x + 4) % 4) * 4 + (z - 2 * core + 4) % 4
    low, high = pick(LOW, role), pick(HIGH, role)

    def remote(src, dst, send, recv, device):
        return pltpu.make_async_remote_copy(
            src_ref=src, dst_ref=dst, send_sem=send, recv_sem=recv, device_id=device, device_id_type=MESH
        )

    def frames_of(place):
        chip = (x + place % 4) % 4
        half = core if place < 4 else 1 - core
        return pl.multiple_of(chip * 256 + half * 128, 128)

    def sv_load(place):
        return pltpu.make_async_copy(
            solved.at[:, pl.ds(frames_of(place), 128)], sv.at[:, pl.ds(place * 128, 128)], sv_sem.at[place]
        )

    fv_load = pltpu.make_async_copy(factor.at[pl.ds(0, KB)], fv.at[pl.ds(0, KB)], load_sem.at[0])
    fv_rest = pltpu.make_async_copy(factor.at[pl.ds(KB, 3 * KB)], fv.at[pl.ds(KB, 3 * KB)], load_sem.at[1])
    fe_load = pltpu.make_async_copy(features.at[pl.ds(frames_of(0), 128)], fe, load_sem.at[2])
    dv_load = pltpu.make_async_copy(dinv, dv, load_sem.at[3])
    acc_load = pltpu.make_async_copy(covariance, acc, load_sem.at[4])

    fv_load.start()
    for place in (4, 5, 6, 7, 0, 1, 2, 3):
        sv_load(place).start()
    fv_rest.start()
    fe_load.start()
    dv_load.start()
    acc_load.start()

    barrier = pltpu.get_barrier_semaphore()
    for device in (sibling,) + along + around:
        pl.semaphore_signal(barrier, inc=1, device_id=device, device_id_type=MESH)

    def rows_of(k):
        return pl.ds(pl.multiple_of(k * KB, KB), KB)

    def sib_copy(k):
        return remote(sib_out.at[k], sib_in.at[k], sib_s.at[k], sib_r.at[k], sibling)

    def red_copy(k, m):
        return remote(red_out.at[k, m], red_in.at[k, m], red_s.at[k, m], red_r.at[k, m], along[m])

    def part_sibling(k):
        sib_out[k] = jnp.dot(fv[rows_of(k), :], sv[:, 512:], preferred_element_type=F32).astype(BF16)
        sib_copy(k).start()

    def part_own(k):
        own[k] = jnp.dot(fv[rows_of(k), :], sv[:, :512], preferred_element_type=F32)

    def reduce(k):
        sib_copy(k).wait_recv()
        for m, first in ((2, 256), (0, 128), (1, 384)):
            piece_cols = pl.ds(first, 128)
            red_out[k, m] = (own[k, :, piece_cols] + sib_in[k, :, piece_cols].astype(F32)).astype(BF16)
            red_copy(k, m).start()
        own[k, :, :128] = own[k, :, :128] + sib_in[k, :, :128].astype(F32)

    def piece(k, chip, half):
        return panels.at[k, 8 + (chip + 4) % 4, pl.ds(pl.multiple_of(half * 128, 128), 128)]

    def gather_copy(k, m):
        chip = (x, x, x, None, x, x - 1, x + 1, x + 2)[m]
        ref = piece(k, chip, core)
        return remote(ref, ref, gat_s.at[k, m], gat_r.at[k, m], along[m] if m < 3 else sibling)

    def make_panel(k):
        @pl.when(k == 0)
        def _():
            fe_load.wait()
            dv_load.wait()
            acc_load.wait()

        for m in range(3):
            red_copy(k, m).wait_recv()
        summed = own[k, :, :128] + red_in[k, 0].astype(F32) + red_in[k, 1].astype(F32) + red_in[k, 2].astype(F32)
        cols = pl.ds(pl.multiple_of(k * KB, KB), KB)
        res[:, cols] = (fe[:, cols].astype(F32) - summed.T).astype(BF16)
        panel = lax.dot_general(res[...], dv[rows_of(k), :], NT, preferred_element_type=F32)
        panels[k, 8 + x, pl.ds(pl.multiple_of(core * 128, 128), 128)] = panel.astype(BF16)
        for m in (4, 0, 1, 2):
            gather_copy(k, m).start()

    def from_along(m):
        def stage(k):
            gather_copy(k, m).wait_recv()
            gather_copy(k, m + 5).start()
        return stage

    def row_done(k):
        for m in range(4, 8):
            gather_copy(k, m).wait_recv()

    def tree_copy(k, u, d, src):
        return remote(panels.at[k, src], panels.at[k, u], tree_s.at[k, u, d], tree_r.at[k, u], around[d])

    def place_of(u):
        return jnp.where(u // 4 == role, 8 + (x + u % 4) % 4, u)

    def passes(u, d):
        word = jnp.where(u < 4, low, high)
        return (lax.shift_right_logical(word, (u % 4) * 4 + d) & 1) == 1

    def hand_on(k, u):
        for d in range(4):
            @pl.when(passes(u, d))
            def _():
                tree_copy(k, u, d, place_of(u)).start()

    def use(k, u):
        first = pl.multiple_of((u // 4) * 1024 + ((x + u % 4) % 4) * 256, 256)
        rows = panels[k, 8:12].reshape(1024, KB)
        acc[:, pl.ds(first, 256)] += lax.dot_general(
            rows, panels[k, place_of(u)], NT, preferred_element_type=F32
        )

    words = tuple(pick([line[index] for line in STEPS], role) for index in range(len(STEPS[0])))
    res[...] = jnp.zeros_like(res)
    fv_load.wait()
    for place in (4, 5, 6, 7):
        sv_load(place).wait()
    pl.semaphore_wait(barrier, 8)
    part_sibling(0)
    for place in (0, 1, 2, 3):
        sv_load(place).wait()
    part_own(0)
    fv_rest.wait()

    stages = (
        part_sibling, part_own, reduce, make_panel, from_along(0), from_along(1), from_along(2), row_done,
    )

    def step(place, word):
        code = lax.shift_right_logical(word, 7 * place) & 127
        k, kind = code // 32, code % 32

        @pl.when(jnp.logical_and(kind >= USE, kind < NOTHING))
        def _():
            use(k, kind - USE)

        @pl.when(jnp.logical_and(kind >= PASS, kind < USE))
        def _():
            tree_copy(k, kind - PASS, 0, kind - PASS).wait_recv()
            hand_on(k, kind - PASS)

        @pl.when(kind < PASS)
        def _():
            for index, stage in enumerate(stages):
                @pl.when(kind == index)
                def _():
                    stage(k)

            for j, m in enumerate((4, 6, 7, 5)):
                @pl.when(kind == SOURCE + j)
                def _():
                    gather_copy(k, m).wait_recv()
                    hand_on(k, role * 4 + j)

        return word

    def four_steps(_, line):
        lax.fori_loop(0, 4, step, line[0])
        return line[1:] + line[:1]

    lax.fori_loop(0, len(words), four_steps, words)

    @pl.loop(0, CHUNKS * 8)
    def _(t):
        k, u = t // 8, t % 8
        for d in range(4):
            @pl.when(passes(u, d))
            def _():
                tree_copy(k, u, d, u).wait_send()

    @pl.loop(0, CHUNKS)
    def _(k):
        sib_copy(k).wait_send()
        for m in range(3):
            red_copy(k, m).wait_send()
        for m in (0, 1, 2, 4, 5, 6, 7):
            gather_copy(k, m).wait_send()


def body(solved, factor_rows, diag_inverse, features, covariance):
    any_place = pl.BlockSpec(memory_space=pl.ANY)
    dma = pltpu.SemaphoreType.DMA
    return pl.pallas_call(
        kernel,
        out_shape=pltpu.VMEM((1024, 2048), F32),
        in_specs=[any_place] * 5,
        out_specs=pl.BlockSpec(memory_space=pltpu.VMEM),
        scratch_shapes=[
            pltpu.VMEM((1024, 1024), BF16),
            pltpu.VMEM((1024, 1024), BF16),
            pltpu.VMEM((1024, 1024), BF16),
            pltpu.VMEM((128, 1024), BF16),
            pltpu.VMEM((128, 1024), BF16),
            pltpu.VMEM((CHUNKS, KB, 512), F32),
            pltpu.VMEM((CHUNKS, KB, 512), BF16),
            pltpu.VMEM((CHUNKS, KB, 512), BF16),
            pltpu.VMEM((CHUNKS, 3, KB, 128), BF16),
            pltpu.VMEM((CHUNKS, 3, KB, 128), BF16),
            pltpu.VMEM((CHUNKS, 12, 256, KB), BF16),
            dma((5,)),
            dma((8,)),
            dma((CHUNKS,)),
            dma((CHUNKS,)),
            dma((CHUNKS, 3)),
            dma((CHUNKS, 3)),
            dma((CHUNKS, 8)),
            dma((CHUNKS, 8)),
            dma((CHUNKS, 8, 4)),
            dma((CHUNKS, 8)),
        ],
        compiler_params=pltpu.CompilerParams(
            collective_id=0, has_side_effects=True, vmem_limit_bytes=44 * 2**20
        ),
        cost_estimate=pl.CostEstimate(flops=7 * 10**9, bytes_accessed=24 * 10**6, transcendentals=0),
    )(solved, factor_rows, diag_inverse, features, covariance)


def solution(mesh):
    placed = (P("col", "row"), P(None, "col"), P(), P("row", None), P("row", "col"))
    return jax.shard_map(
        body, mesh=mesh, in_specs=placed, out_specs=P("row", "col"), check_vma=False
    )
```

```python
import jax
import jax.numpy as jnp
from jax import lax
from jax.experimental import pallas as pl
from jax.experimental.pallas import tpu as pltpu
from jax.sharding import PartitionSpec as P

F32 = jnp.float32
BF16 = jnp.bfloat16
CHUNKS = 4
KB = 256
NT = (((1,), (1,)), ((), ()))
MESH = pl.DeviceIdType.MESH

(
    PART_SIBLING, PART_OWN, REDUCE, PANEL, FROM_PREV, FROM_NEXT, FROM_OPPOSITE, ROW_DONE,
) = range(8)
SOURCE, PASS, USE, DRAIN, OTHERS, NOTHING = 8, 12, 20, 28, 30, 31
MASKS = (
    (3994502, 32776, 3470214, 32776, 3994502, 32776, 3994502, 32776),
    (1073216, 1373067, 1074240, 1373067, 1073216, 1373067, 1073216, 1373067),
    (12288, 320, 12416, 320, 12288, 320, 12288, 320),
    (0, 528392, 0, 528392, 0, 528392, 0, 528392),
    (3457536, 2887680, 7651840, 2887680, 3457536, 2887680, 3457536, 2887680),
    (1049344, 3444748, 1050368, 3444748, 1049344, 3444748, 1049348, 3444748),
    (128, 324, 128, 324, 128, 324, 128, 324),
    (4098, 786688, 4098, 786688, 4098, 786688, 4198402, 786688),
    (3162126, 295424, 3162126, 295424, 3162126, 295424, 3162126, 295424),
    (1327107, 1311372, 1327107, 1311372, 1327107, 1311372, 1327107, 1311372),
    (2, 270341, 2, 270341, 2, 270341, 0, 270341),
    (522, 1, 522, 1, 522, 1, 522, 1),
    (2139018, 0, 2138762, 0, 2106250, 0, 41866, 0),
    (384, 49546, 0, 49546, 384, 49546, 384, 49546),
    (1, 24832, 1, 24832, 16385, 24832, 1, 24832),
    (2097288, 256, 2097288, 256, 2097288, 256, 2097288, 256),
)
STEPS = (
    (134254752, 205004962, 74485507, 84029758, 198231179, 21682192, 46418580, 53103639, 90157512, 112004370, 219342006, 118351153, 225798713, 222619753, 185985819, 122469108, 125065718, 253508569, 255618386, 192216434, 258947484, 65535580, 65523615, 65523615, 65523615, 65523615),
    (134254752, 205004962, 74485507, 84029758, 198231179, 21681676, 48483348, 27938073, 208801173, 111122346, 153996046, 156120139, 111893817, 161150139, 97924436, 162966710, 167652821, 259964119, 181647980, 127793052, 249281261, 65535580, 65523615, 65523615, 65523615, 65523615),
    (134254752, 205004962, 74485507, 15003966, 53971139, 265869723, 124160295, 34360207, 105800600, 25958330, 30274452, 118298134, 192212177, 190089869, 259849457, 177421682, 183753518, 164326480, 251390773, 253508462, 179534444, 246363804, 65535580, 65523615, 65523615, 65523615),
    (134254752, 205004962, 74485507, 14938430, 44265283, 101058583, 99221347, 52714551, 149637902, 38639413, 179532698, 56945615, 42150734, 120355823, 124582637, 109784144, 122469230, 253504721, 190102769, 257732051, 241642060, 245046907, 65535580, 65523615, 65523615, 65523615),
    (134254752, 205004962, 74485507, 8483134, 79143302, 48351140, 145098790, 265023920, 142968595, 147705255, 93194764, 98120372, 124625843, 166103398, 216352471, 185871182, 251387186, 249277907, 252082193, 190097996, 242948781, 104644084, 179535161, 171800220, 127826137, 65535580),
    (134254752, 205004962, 74485507, 8483134, 35103110, 40441893, 57248775, 32305605, 54823934, 124654532, 168117958, 185725541, 36483887, 46373785, 192535891, 251987568, 110401070, 166423862, 181644213, 259841201, 251395442, 163293772, 187988821, 237452013, 245046905, 65535580),
    (134254752, 205004962, 74485507, 8483134, 140624677, 75902736, 118084400, 146780563, 143018139, 124576710, 48493157, 44266470, 120351824, 42146735, 109784531, 253496078, 94678225, 183753370, 259849457, 251387186, 162732846, 190098132, 246789838, 228439836, 127842676, 65535580),
    (134254752, 205004962, 74485507, 8483134, 140624677, 82416222, 146328463, 143001726, 118609990, 211377071, 217681299, 46369292, 114003089, 109780403, 44264399, 181644368, 251387057, 192204050, 249277004, 111901808, 255618257, 259841330, 190102124, 257259853, 127760028, 65535580),
    (134254752, 205004962, 74485507, 10563902, 77046150, 142803877, 208343828, 145082366, 33774119, 101059270, 100217528, 214279054, 95276177, 216451509, 124578380, 54827822, 183757517, 245046449, 122465360, 251390798, 192215789, 190098641, 253508462, 241646833, 257728123, 65535580),
    (134254752, 205004962, 74485507, 10563902, 77046150, 142869413, 208409368, 36784638, 117887897, 92611340, 108606132, 49399739, 27702034, 120353685, 122542383, 184920078, 192227788, 253504721, 114120366, 183757517, 190102769, 164051564, 230615923, 251492719, 249273978, 65535580),
    (134254752, 205004962, 74485507, 10563902, 140624676, 82416350, 145833827, 101813264, 56941639, 217690725, 109775372, 124148113, 48483602, 103533197, 122461367, 168512270, 175320117, 190098900, 170638448, 238283958, 179535063, 227786098, 230488662, 251395573, 248461084, 65535580),
    (134254752, 205004962, 74485507, 10563902, 140624676, 82416350, 145833827, 93424140, 209967687, 50606743, 44266470, 116120624, 56937617, 177412781, 54823694, 183753518, 179526833, 245046707, 169565490, 186379086, 187988981, 173468144, 238795866, 259849462, 256850204, 65535580),
    (134254752, 205004962, 74485507, 8483134, 26714502, 32052773, 34685837, 48583444, 102729571, 50973508, 111895348, 213070392, 96774727, 99463962, 217406413, 185985103, 122468972, 52718414, 250017683, 253508333, 125089587, 239893338, 187989305, 237448659, 259849404, 65535580),
    (134254752, 205004962, 74485507, 8483134, 35103110, 36247589, 53562375, 39825830, 118088218, 103910029, 213461049, 105180231, 30323483, 170232332, 187504231, 252631536, 49498066, 255618389, 99335538, 177413046, 175860558, 111901403, 232467407, 259849076, 250558364, 65535580),
    (134254752, 205004962, 74485507, 8483134, 140624677, 82416222, 265373923, 43058713, 110220870, 213454098, 45713293, 34360295, 118234264, 56941874, 188033228, 190094771, 46917262, 167537335, 228375767, 97921140, 192216374, 111901421, 234077296, 249281494, 127859100, 65535580),
    (134254752, 205004962, 74485507, 8483134, 140624677, 43487756, 109695788, 146780559, 45155991, 46375878, 52720229, 216888109, 54831692, 116120366, 51599504, 101968569, 227449906, 56949335, 247164113, 190102382, 251387315, 257735921, 185871827, 165558300, 259841622, 65535580),
)


def pick(table, role):
    value = jnp.asarray(table[0], jnp.int32)
    for index in range(1, len(table)):
        value = jnp.where(role == index, jnp.asarray(table[index], jnp.int32), value)
    return value


def kernel(
    solved, factor, dinv, features, covariance, acc,
    sv, fv, dv, fe, res, own, sib_out, sib_in, red_out, red_in, panels,
    load_sem, sv_sem, sib_s, sib_r, red_s, red_r, gat_s, gat_r, tree_s, tree_r,
):
    row = lax.axis_index("row")
    col = lax.axis_index("col")
    y, z = row // 4, row % 4
    x, core = col // 2, col % 2

    def at(xx, yy, zz, cc):
        return {"row": ((yy + 4) % 4) * 4 + (zz + 4) % 4, "col": ((xx + 4) % 4) * 2 + cc}

    sibling = at(x, y, z, 1 - core)
    along = (at(x + 1, y, z, core), at(x - 1, y, z, core), at(x + 2, y, z, core))
    around = (
        at(x, y + 1, z, core), at(x, y - 1, z, core), at(x, y, z + 1, core), at(x, y, z - 1, core),
        at(x, y + 2, z, core), at(x, y, z + 2, core),
    )

    ahead = (y - x + 4) % 4
    role = ahead * 4 + (z - 2 * core + 4) % 4
    masks = [pick([line[index] for line in MASKS], role) for index in range(2 * CHUNKS)]

    def remote(src, dst, send, recv, device):
        return pltpu.make_async_remote_copy(
            src_ref=src, dst_ref=dst, send_sem=send, recv_sem=recv, device_id=device, device_id_type=MESH
        )

    def frames_of(place):
        chip = (x + place % 4) % 4
        half = core if place < 4 else 1 - core
        return pl.multiple_of(chip * 256 + half * 128, 128)

    def sv_load(place):
        return pltpu.make_async_copy(
            solved.at[:, pl.ds(frames_of(place), 128)], sv.at[:, pl.ds(place * 128, 128)], sv_sem.at[place]
        )

    fv_load = pltpu.make_async_copy(factor.at[pl.ds(0, KB)], fv.at[pl.ds(0, KB)], load_sem.at[0])
    fv_rest = pltpu.make_async_copy(factor.at[pl.ds(KB, 3 * KB)], fv.at[pl.ds(KB, 3 * KB)], load_sem.at[1])
    fe_load = pltpu.make_async_copy(features.at[pl.ds(frames_of(0), 128)], fe, load_sem.at[2])
    dv_load = pltpu.make_async_copy(dinv, dv, load_sem.at[3])
    acc_load = pltpu.make_async_copy(covariance, acc, load_sem.at[4])

    fv_load.start()
    for place in (4, 5, 6, 7, 0, 1, 2, 3):
        sv_load(place).start()
    fv_rest.start()
    fe_load.start()
    dv_load.start()
    acc_load.start()

    barrier = pltpu.get_barrier_semaphore()
    for device in (sibling,) + along + around:
        pl.semaphore_signal(barrier, inc=1, device_id=device, device_id_type=MESH)

    def rows_of(k):
        return pl.ds(pl.multiple_of(k * KB, KB), KB)

    def sib_copy(k):
        return remote(sib_out.at[k], sib_in.at[k], sib_s.at[k], sib_r.at[k], sibling)

    def red_copy(k, m):
        return remote(red_out.at[k, m], red_in.at[k, m], red_s.at[k, m], red_r.at[k, m], along[m])

    def part_sibling(k, ready=lambda: None):
        sib_out[k] = jnp.dot(fv[rows_of(k), :], sv[:, 512:], preferred_element_type=F32).astype(BF16)
        ready()
        sib_copy(k).start()

    def part_own(k):
        own[k] = jnp.dot(fv[rows_of(k), :], sv[:, :512], preferred_element_type=F32)

    def reduce(k):
        sib_copy(k).wait_recv()
        for m, first in ((2, 256), (0, 128), (1, 384)):
            piece_cols = pl.ds(first, 128)
            red_out[k, m] = (own[k, :, piece_cols] + sib_in[k, :, piece_cols].astype(F32)).astype(BF16)
            red_copy(k, m).start()
        own[k, :, :128] = own[k, :, :128] + sib_in[k, :, :128].astype(F32)

    def piece(k, chip, half):
        return panels.at[k, 8 + (chip + 4) % 4, pl.ds(pl.multiple_of(half * 128, 128), 128)]

    def gather_copy(k, m):
        chip = (x, x, x, None, x, x - 1, x + 1, x + 2)[m]
        ref = piece(k, chip, core)
        return remote(ref, ref, gat_s.at[k, m], gat_r.at[k, m], along[m] if m < 3 else sibling)

    def first_copy(k):
        ref = piece(k, x, core)
        slot = jnp.where(ahead == 1, 0, jnp.where(ahead == 3, 1, 2)) + jnp.where(core == z // 2, 0, 5)
        return remote(ref, ref, gat_s.at[k, 3], gat_r.at[k, slot], at(y, y, z, z // 2))

    def whole_copy(k, m):
        ref = panels.at[k, 8 + (x + (3, 1, 2)[m]) % 4]
        return remote(ref, ref, gat_s.at[k, m + 5], gat_r.at[k, m + 5], sibling)

    def others(k, do):
        for m, steps in enumerate((1, 3, 2)):
            @pl.when(ahead != steps)
            def _():
                do(gather_copy(k, m))

    def make_panel(k):
        @pl.when(k == 0)
        def _():
            fe_load.wait()
            dv_load.wait()
            acc_load.wait()

        for m in range(3):
            red_copy(k, m).wait_recv()
        summed = own[k, :, :128] + red_in[k, 0].astype(F32) + red_in[k, 1].astype(F32) + red_in[k, 2].astype(F32)
        cols = pl.ds(pl.multiple_of(k * KB, KB), KB)
        res[:, cols] = (fe[:, cols].astype(F32) - summed.T).astype(BF16)
        panel = lax.dot_general(res[...], dv[rows_of(k), :], NT, preferred_element_type=F32)
        panels[k, 8 + x, pl.ds(pl.multiple_of(core * 128, 128), 128)] = panel.astype(BF16)
        @pl.when(ahead != 0)
        def _():
            first_copy(k).start()

        gather_copy(k, 4).start()

    def from_along(m):
        def stage(k):
            gather_copy(k, m).wait_recv()
            gather_copy(k, m + 5).start()
        return stage

    def row_done(k):
        gather_copy(k, 4).wait_recv()

        @pl.when(ahead != 0)
        def _():
            for m in range(3):
                gather_copy(k, m + 5).wait_recv()

        @pl.when(ahead == 0)
        def _():
            for m in range(3):
                whole_copy(k, m).wait_recv()

    def tree_copy(k, u, d, src):
        return remote(panels.at[k, src], panels.at[k, u], tree_s.at[k, u, d], tree_r.at[k, u], around[d])

    def place_of(u):
        return jnp.where(u // 4 == role, 8 + (x + u % 4) % 4, u)

    def each_way(k, u, do):
        bits = lax.shift_right_logical(pick(masks, 2 * k + u // 4), (u % 4) * 6) & 63
        for d in range(6):
            @pl.when((lax.shift_right_logical(bits, d) & 1) == 1)
            def _():
                do(d)

    def hand_on(k, u):
        each_way(k, u, lambda d: tree_copy(k, u, d, place_of(u)).start())

    def drain(k):
        @pl.loop(0, 8)
        def _(u):
            each_way(k, u, lambda d: tree_copy(k, u, d, u).wait_send())

        sib_copy(k).wait_send()
        for m in range(3):
            red_copy(k, m).wait_send()
        gather_copy(k, 4).wait_send()
        others(k, lambda copy: copy.wait_send())

        @pl.when(ahead != 0)
        def _():
            first_copy(k).wait_send()
            for m in range(3):
                gather_copy(k, m + 5).wait_send()

        @pl.when(role < 2)
        def _():
            for m in range(3):
                whole_copy(k, m).wait_send()

    def use(k, u):
        first = pl.multiple_of((u // 4) * 1024 + ((x + u % 4) % 4) * 256, 256)
        rows = panels[k, 8:12].reshape(1024, KB)
        acc[:, pl.ds(first, 256)] += lax.dot_general(
            rows, panels[k, place_of(u)], NT, preferred_element_type=F32
        )

    words = tuple(pick([line[index] for line in STEPS], role) for index in range(len(STEPS[0])))
    res[...] = jnp.zeros_like(res)
    fv_load.wait()
    for place in (4, 5, 6, 7):
        sv_load(place).wait()
    for place in (0, 1, 2, 3):
        sv_load(place).wait()
    part_own(0)
    part_sibling(0, lambda: pl.semaphore_wait(barrier, 10))
    fv_rest.wait()

    stages = (
        part_sibling, part_own, reduce, make_panel, from_along(0), from_along(1), from_along(2), row_done,
    )

    def step(place, word):
        code = lax.shift_right_logical(word, 7 * place) & 127
        k, kind = code // 32, code % 32

        @pl.when(jnp.logical_and(kind >= USE, kind < DRAIN))
        def _():
            use(k, kind - USE)

        @pl.when(jnp.logical_and(kind >= PASS, kind < USE))
        def _():
            tree_copy(k, kind - PASS, 0, kind - PASS).wait_recv()
            hand_on(k, kind - PASS)

        @pl.when(kind < PASS)
        def _():
            for index, stage in enumerate(stages):
                @pl.when(kind == index)
                def _():
                    stage(k)

            @pl.when(kind == SOURCE)
            def _():
                gather_copy(k, 4).wait_recv()
                hand_on(k, role * 4)

            for j, m in ((1, 1), (2, 2), (3, 0)):
                @pl.when(kind == SOURCE + j)
                def _():
                    gather_copy(k, m).wait_recv()
                    gather_copy(k, m + 5).wait_recv()
                    hand_on(k, role * 4 + j)
                    whole_copy(k, m).start()

        @pl.when(kind == DRAIN)
        def _():
            drain(k)

        @pl.when(kind == OTHERS)
        def _():
            others(k, lambda copy: copy.start())

        return word

    def four_steps(_, line):
        lax.fori_loop(0, 4, step, line[0])
        return line[1:] + line[:1]

    lax.fori_loop(0, len(words), four_steps, words)


def body(solved, factor_rows, diag_inverse, features, covariance):
    any_place = pl.BlockSpec(memory_space=pl.ANY)
    dma = pltpu.SemaphoreType.DMA
    return pl.pallas_call(
        kernel,
        out_shape=pltpu.VMEM((1024, 2048), F32),
        in_specs=[any_place] * 5,
        out_specs=pl.BlockSpec(memory_space=pltpu.VMEM),
        scratch_shapes=[
            pltpu.VMEM((1024, 1024), BF16),
            pltpu.VMEM((1024, 1024), BF16),
            pltpu.VMEM((1024, 1024), BF16),
            pltpu.VMEM((128, 1024), BF16),
            pltpu.VMEM((128, 1024), BF16),
            pltpu.VMEM((CHUNKS, KB, 512), F32),
            pltpu.VMEM((CHUNKS, KB, 512), BF16),
            pltpu.VMEM((CHUNKS, KB, 512), BF16),
            pltpu.VMEM((CHUNKS, 3, KB, 128), BF16),
            pltpu.VMEM((CHUNKS, 3, KB, 128), BF16),
            pltpu.VMEM((CHUNKS, 12, 256, KB), BF16),
            dma((5,)),
            dma((8,)),
            dma((CHUNKS,)),
            dma((CHUNKS,)),
            dma((CHUNKS, 3)),
            dma((CHUNKS, 3)),
            dma((CHUNKS, 8)),
            dma((CHUNKS, 8)),
            dma((CHUNKS, 8, 6)),
            dma((CHUNKS, 8)),
        ],
        compiler_params=pltpu.CompilerParams(
            collective_id=0, has_side_effects=True, vmem_limit_bytes=44 * 2**20
        ),
        cost_estimate=pl.CostEstimate(flops=7 * 10**9, bytes_accessed=24 * 10**6, transcendentals=0),
    )(solved, factor_rows, diag_inverse, features, covariance)


def solution(mesh):
    placed = (P("col", "row"), P(None, "col"), P(), P("row", None), P("row", "col"))
    return jax.shard_map(
        body, mesh=mesh, in_specs=placed, out_specs=P("row", "col"), check_vma=False
    )
```

```python
import jax
import jax.numpy as jnp
from jax import lax
from jax.experimental import pallas as pl
from jax.experimental.pallas import tpu as pltpu
from jax.sharding import PartitionSpec as P

F32 = jnp.float32
BF16 = jnp.bfloat16
CHUNKS = 4
KB = 256
NT = (((1,), (1,)), ((), ()))
MESH = pl.DeviceIdType.MESH

(
    PART_SIBLING, PART_OWN, REDUCE, PANEL, FROM_PREV, FROM_NEXT, FROM_OPPOSITE, ROW_DONE,
) = range(8)
SOURCE, PASS, USE, DRAIN, OTHERS, NOTHING = 8, 12, 20, 28, 30, 31
MASKS = (
    (1597889, 137, 1847426, 2097155, 1348417, 529026, 2937731, 2920458),
    (1597440, 2400655, 1048576, 2642507, 1597826, 1876615, 8258, 3191241),
    (136, 16643, 524608, 24577, 1048640, 1310784, 2359300, 786560),
    (262656, 2359360, 0, 2097160, 8192, 1573376, 2404480, 4096),
    (589, 295040, 2113540, 40968, 2413069, 778, 20493, 1310729),
    (2097156, 2359553, 16385, 2134849, 24578, 278540, 21314, 21257),
    (33283, 4, 2363392, 384, 4675, 1048577, 385, 1057024),
    (32899, 33025, 2629632, 32896, 2101321, 1048579, 4104, 262273),
    (58117, 2105856, 33418, 2101248, 2379777, 128, 3149828, 512),
    (1573120, 1368960, 132, 2654540, 524288, 2122496, 787264, 33541),
    (1572992, 802880, 1048578, 540932, 8, 1069120, 0, 16386),
    (45121, 4160, 8322, 524608, 65, 8197, 32768, 0),
    (532740, 10, 2646414, 32776, 2097280, 41472, 2621448, 2097728),
    (1589252, 2121864, 553413, 3670532, 1573504, 1089670, 16384, 541316),
    (1048576, 1052674, 2118081, 1613824, 524288, 528384, 524289, 2646021),
    (266240, 278528, 1, 513, 33289, 4224, 2097802, 16384),
)
STEPS = (
    (134254752, 205004962, 17862403, 85499683, 100926603, 140823050, 90533704, 50713750, 54826267, 219732660, 156391934, 103671222, 177134776, 182086379, 244709482, 249392337, 253143415, 259845200, 257727794, 192203921, 60710513, 65535580, 65523615, 65523615, 65523615, 65523615),
    (134254752, 205004962, 17862403, 85499683, 50496651, 198320527, 48941709, 57052329, 30301226, 265957782, 116122953, 185523531, 188406316, 223802586, 255732429, 183762426, 26556108, 249281172, 245045933, 181639982, 127782511, 65535580, 65523615, 65523615, 65523615, 65523615),
    (134254752, 205004962, 74485507, 140783934, 265865438, 31869959, 105506839, 42174010, 100017046, 174921271, 241600859, 255622631, 119888013, 183757517, 118234547, 251390540, 249273005, 114015602, 245050577, 247163726, 253496723, 126299474, 65535580, 65523615, 65523615, 65523615),
    (134254752, 205004962, 74485507, 198242622, 16757136, 35980824, 109777817, 124570253, 102065863, 164534584, 100398038, 175864759, 39566043, 248915994, 48495728, 166615249, 46381527, 41729497, 95632667, 190097973, 255613742, 126302828, 65535580, 65523615, 65523615, 65523615),
    (134254752, 205004962, 74485507, 10694974, 197239172, 77923213, 101059216, 80284131, 99024716, 97325996, 143530934, 227812165, 149841585, 210545364, 122925925, 217442262, 233015512, 236784790, 54836343, 48495470, 190093997, 259849457, 187981235, 247168370, 127330716, 65535580),
    (134254752, 205004962, 74485507, 10760510, 13681200, 16222604, 57021076, 80291939, 118085886, 52714674, 122774340, 109787212, 185920071, 215577134, 237227282, 114947607, 124579314, 181648500, 247168377, 116125010, 249273005, 179522189, 259845071, 251391185, 59082556, 65535580),
    (134254752, 205004962, 74485507, 8483134, 75607875, 50451088, 81757795, 82928148, 104425542, 150581817, 159795416, 56947668, 174954287, 33320375, 257735831, 226721267, 244688661, 106260205, 108313274, 118238523, 252033038, 166411247, 112957108, 55855447, 126303065, 65535580),
    (134254752, 205004962, 74485507, 8483134, 25276227, 42062500, 27901795, 51448464, 118232005, 36909766, 210622361, 109785927, 227944532, 244964529, 122464973, 181635854, 183761903, 174937838, 98416731, 48494774, 241600819, 259947579, 247168370, 187977107, 126299474, 65535580),
    (134254752, 205004962, 74485507, 8483134, 25276227, 78187015, 265865260, 44258072, 82578319, 118579764, 30510225, 99010966, 159685604, 149648229, 97852058, 245046119, 181640627, 251387186, 187984847, 253504850, 232062193, 248966224, 256792818, 230619548, 127231733, 65535580),
    (134254752, 205004962, 74485507, 8483134, 33664835, 78187527, 265865392, 40178444, 38391193, 118579738, 28412815, 120350741, 124901860, 123312485, 46379992, 173812945, 93027418, 255613620, 244771308, 163355438, 257272526, 230419407, 160168949, 241642039, 127776635, 65535580),
    (134254752, 205004962, 74485507, 8483134, 14790467, 265867813, 101058598, 36577959, 26288921, 58296851, 38924901, 27641754, 184906704, 122461361, 30207185, 125576726, 95856980, 116128821, 191703468, 114015731, 257849586, 251394668, 181647004, 162916341, 127773422, 65535580),
    (134254752, 205004962, 74485507, 8483134, 14790467, 26792485, 92607358, 147937831, 33900228, 211399320, 36822064, 159745817, 56947668, 111889682, 114002831, 124578896, 120355436, 251390669, 181640498, 173402012, 100513626, 246282477, 192686585, 187988344, 127860083, 65535580),
    (134254752, 205004962, 74485507, 10563902, 14131628, 48351120, 44257956, 207820824, 29985406, 109696918, 111895236, 97623095, 211383862, 214885299, 216451567, 229948404, 246852172, 255622256, 104049873, 106179385, 185951930, 183762419, 54937873, 249277907, 126303602, 65535580),
    (134254752, 205004962, 74485507, 8663358, 198236165, 50448518, 53154468, 33082642, 168153982, 82627213, 26026692, 47286036, 56944824, 211071675, 95841351, 189622758, 255457499, 115120302, 122469689, 183757517, 116128880, 259844684, 226966382, 127121396, 247167958, 65535580),
    (134254752, 205004962, 74485507, 10563902, 33664835, 78187527, 81768880, 145822636, 117868852, 210094022, 185725648, 37329330, 42147097, 216976787, 116116238, 192207533, 114015731, 257735276, 251395313, 28601295, 182200085, 160742489, 247164244, 249273521, 126298829, 65535580),
    (134254752, 205004962, 74485507, 10563902, 14790467, 34280100, 80101219, 145824295, 26319920, 116126228, 28943333, 216266261, 124582423, 251382929, 56985998, 173222734, 190126765, 245806738, 185440080, 104638961, 192309433, 232680141, 256809334, 259930608, 127264668, 65535580),
)


def pick(table, role):
    value = jnp.asarray(table[0], jnp.int32)
    for index in range(1, len(table)):
        value = jnp.where(role == index, jnp.asarray(table[index], jnp.int32), value)
    return value


def kernel(
    solved, factor, dinv, features, covariance, acc,
    sv, fv, dv, fe, res, own, sib_out, sib_in, red_out, red_in, panels,
    load_sem, sv_sem, sib_s, sib_r, red_s, red_r, gat_s, gat_r, tree_s, tree_r,
):
    row = lax.axis_index("row")
    col = lax.axis_index("col")
    y, z = row // 4, row % 4
    x, core = col // 2, col % 2

    def at(xx, yy, zz, cc):
        return {"row": ((yy + 4) % 4) * 4 + (zz + 4) % 4, "col": ((xx + 4) % 4) * 2 + cc}

    sibling = at(x, y, z, 1 - core)
    along = (at(x + 1, y, z, core), at(x - 1, y, z, core), at(x + 2, y, z, core))
    around = (
        at(x, y + 1, z, core), at(x, y - 1, z, core), at(x, y, z + 1, core), at(x, y, z - 1, core),
        at(x, y + 2, z, core), at(x, y, z + 2, core),
    )

    ahead = (y - x + 4) % 4
    role = ahead * 4 + (z - 2 * core + 4) % 4
    masks = [pick([line[index] for line in MASKS], role) for index in range(2 * CHUNKS)]

    def remote(src, dst, send, recv, device):
        return pltpu.make_async_remote_copy(
            src_ref=src, dst_ref=dst, send_sem=send, recv_sem=recv, device_id=device, device_id_type=MESH
        )

    def frames_of(place):
        chip = (x + place % 4) % 4
        half = core if place < 4 else 1 - core
        return pl.multiple_of(chip * 256 + half * 128, 128)

    def sv_load(place):
        return pltpu.make_async_copy(
            solved.at[:, pl.ds(frames_of(place), 128)], sv.at[:, pl.ds(place * 128, 128)], sv_sem.at[place]
        )

    fv_load = pltpu.make_async_copy(factor.at[pl.ds(0, KB)], fv.at[pl.ds(0, KB)], load_sem.at[0])
    fv_rest = pltpu.make_async_copy(factor.at[pl.ds(KB, 3 * KB)], fv.at[pl.ds(KB, 3 * KB)], load_sem.at[1])
    fe_load = pltpu.make_async_copy(features.at[pl.ds(frames_of(0), 128)], fe, load_sem.at[2])
    dv_load = pltpu.make_async_copy(dinv, dv, load_sem.at[3])
    acc_load = pltpu.make_async_copy(covariance, acc, load_sem.at[4])

    fv_load.start()
    for place in (4, 5, 6, 7, 0, 1, 2, 3):
        sv_load(place).start()
    fv_rest.start()
    fe_load.start()
    dv_load.start()
    acc_load.start()

    barrier = pltpu.get_barrier_semaphore()
    for device in (sibling,) + along + around:
        pl.semaphore_signal(barrier, inc=1, device_id=device, device_id_type=MESH)

    def rows_of(k):
        return pl.ds(pl.multiple_of(k * KB, KB), KB)

    def sib_copy(k):
        return remote(sib_out.at[k], sib_in.at[k], sib_s.at[k], sib_r.at[k], sibling)

    def red_copy(k, m):
        return remote(red_out.at[k, m], red_in.at[k, m], red_s.at[k, m], red_r.at[k, m], along[m])

    def part_sibling(k, ready=lambda: None):
        sib_out[k] = jnp.dot(fv[rows_of(k), :], sv[:, 512:], preferred_element_type=F32).astype(BF16)
        ready()
        sib_copy(k).start()

    def part_own(k):
        own[k] = jnp.dot(fv[rows_of(k), :], sv[:, :512], preferred_element_type=F32)

    def reduce(k):
        sib_copy(k).wait_recv()
        for m, first in ((2, 256), (0, 128), (1, 384)):
            piece_cols = pl.ds(first, 128)
            red_out[k, m] = (own[k, :, piece_cols] + sib_in[k, :, piece_cols].astype(F32)).astype(BF16)
            red_copy(k, m).start()
        own[k, :, :128] = own[k, :, :128] + sib_in[k, :, :128].astype(F32)

    def piece(k, chip, half):
        return panels.at[k, 8 + (chip + 4) % 4, pl.ds(pl.multiple_of(half * 128, 128), 128)]

    def gather_copy(k, m):
        chip = (x, x, x, None, x, x - 1, x + 1, x + 2)[m]
        ref = piece(k, chip, core)
        return remote(ref, ref, gat_s.at[k, m], gat_r.at[k, m], along[m] if m < 3 else sibling)

    def first_copy(k):
        ref = piece(k, x, core)
        slot = jnp.where(ahead == 1, 0, jnp.where(ahead == 3, 1, 2)) + jnp.where(core == z // 2, 0, 5)
        return remote(ref, ref, gat_s.at[k, 3], gat_r.at[k, slot], at(y, y, z, z // 2))

    def whole_copy(k, m):
        ref = panels.at[k, 8 + (x + (3, 1, 2)[m]) % 4]
        return remote(ref, ref, gat_s.at[k, m + 5], gat_r.at[k, m + 5], sibling)

    def others(k, do):
        for m, steps in enumerate((1, 3, 2)):
            @pl.when(ahead != steps)
            def _():
                do(gather_copy(k, m))

    def make_panel(k):
        @pl.when(k == 0)
        def _():
            fe_load.wait()
            dv_load.wait()
            acc_load.wait()

        for m in range(3):
            red_copy(k, m).wait_recv()
        summed = own[k, :, :128] + red_in[k, 0].astype(F32) + red_in[k, 1].astype(F32) + red_in[k, 2].astype(F32)
        cols = pl.ds(pl.multiple_of(k * KB, KB), KB)
        res[:, cols] = (fe[:, cols].astype(F32) - summed.T).astype(BF16)
        panel = lax.dot_general(res[...], dv[rows_of(k), :], NT, preferred_element_type=F32)
        panels[k, 8 + x, pl.ds(pl.multiple_of(core * 128, 128), 128)] = panel.astype(BF16)
        @pl.when(ahead != 0)
        def _():
            first_copy(k).start()

        gather_copy(k, 4).start()

    def from_along(m):
        def stage(k):
            gather_copy(k, m).wait_recv()
            gather_copy(k, m + 5).start()
        return stage

    def row_done(k):
        gather_copy(k, 4).wait_recv()

        @pl.when(ahead != 0)
        def _():
            for m in range(3):
                gather_copy(k, m + 5).wait_recv()

        @pl.when(ahead == 0)
        def _():
            for m in range(3):
                whole_copy(k, m).wait_recv()

    def tree_copy(k, u, d, src):
        return remote(panels.at[k, src], panels.at[k, u], tree_s.at[k, u, d], tree_r.at[k, u], around[d])

    def place_of(u):
        return jnp.where(u // 4 == role, 8 + (x + u % 4) % 4, u)

    def each_way(k, u, do):
        bits = lax.shift_right_logical(pick(masks, 2 * k + u // 4), (u % 4) * 6) & 63
        for d in range(6):
            @pl.when((lax.shift_right_logical(bits, d) & 1) == 1)
            def _():
                do(d)

    def hand_on(k, u):
        each_way(k, u, lambda d: tree_copy(k, u, d, place_of(u)).start())

    def drain(k):
        @pl.loop(0, 8)
        def _(u):
            each_way(k, u, lambda d: tree_copy(k, u, d, u).wait_send())

        sib_copy(k).wait_send()
        for m in range(3):
            red_copy(k, m).wait_send()
        gather_copy(k, 4).wait_send()
        others(k, lambda copy: copy.wait_send())

        @pl.when(ahead != 0)
        def _():
            first_copy(k).wait_send()
            for m in range(3):
                gather_copy(k, m + 5).wait_send()

        @pl.when(role < 2)
        def _():
            for m in range(3):
                whole_copy(k, m).wait_send()

    def use(k, u):
        first = pl.multiple_of((u // 4) * 1024 + ((x + u % 4) % 4) * 256, 256)
        rows = panels[k, 8:12].reshape(1024, KB)
        acc[:, pl.ds(first, 256)] += lax.dot_general(
            rows, panels[k, place_of(u)], NT, preferred_element_type=F32
        )

    words = tuple(pick([line[index] for line in STEPS], role) for index in range(len(STEPS[0])))
    res[...] = jnp.zeros_like(res)
    fv_load.wait()
    for place in (4, 5, 6, 7):
        sv_load(place).wait()
    for place in (0, 1, 2, 3):
        sv_load(place).wait()
    part_own(0)
    part_sibling(0, lambda: pl.semaphore_wait(barrier, 10))
    fv_rest.wait()

    stages = (
        part_sibling, part_own, reduce, make_panel, from_along(0), from_along(1), from_along(2), row_done,
    )

    def step(place, word):
        code = lax.shift_right_logical(word, 7 * place) & 127
        k, kind = code // 32, code % 32

        @pl.when(jnp.logical_and(kind >= USE, kind < DRAIN))
        def _():
            use(k, kind - USE)

        @pl.when(jnp.logical_and(kind >= PASS, kind < USE))
        def _():
            tree_copy(k, kind - PASS, 0, kind - PASS).wait_recv()
            hand_on(k, kind - PASS)

        @pl.when(kind < PASS)
        def _():
            for index, stage in enumerate(stages):
                @pl.when(kind == index)
                def _():
                    stage(k)

            @pl.when(kind == SOURCE)
            def _():
                gather_copy(k, 4).wait_recv()
                hand_on(k, role * 4)

            for j, m in ((1, 1), (2, 2), (3, 0)):
                @pl.when(kind == SOURCE + j)
                def _():
                    gather_copy(k, m).wait_recv()
                    gather_copy(k, m + 5).wait_recv()
                    hand_on(k, role * 4 + j)
                    whole_copy(k, m).start()

        @pl.when(kind == DRAIN)
        def _():
            drain(k)

        @pl.when(kind == OTHERS)
        def _():
            others(k, lambda copy: copy.start())

        return word

    def four_steps(_, line):
        lax.fori_loop(0, 4, step, line[0])
        return line[1:] + line[:1]

    lax.fori_loop(0, len(words), four_steps, words)


def body(solved, factor_rows, diag_inverse, features, covariance):
    any_place = pl.BlockSpec(memory_space=pl.ANY)
    dma = pltpu.SemaphoreType.DMA
    return pl.pallas_call(
        kernel,
        out_shape=pltpu.VMEM((1024, 2048), F32),
        in_specs=[any_place] * 5,
        out_specs=pl.BlockSpec(memory_space=pltpu.VMEM),
        scratch_shapes=[
            pltpu.VMEM((1024, 1024), BF16),
            pltpu.VMEM((1024, 1024), BF16),
            pltpu.VMEM((1024, 1024), BF16),
            pltpu.VMEM((128, 1024), BF16),
            pltpu.VMEM((128, 1024), BF16),
            pltpu.VMEM((CHUNKS, KB, 512), F32),
            pltpu.VMEM((CHUNKS, KB, 512), BF16),
            pltpu.VMEM((CHUNKS, KB, 512), BF16),
            pltpu.VMEM((CHUNKS, 3, KB, 128), BF16),
            pltpu.VMEM((CHUNKS, 3, KB, 128), BF16),
            pltpu.VMEM((CHUNKS, 12, 256, KB), BF16),
            dma((5,)),
            dma((8,)),
            dma((CHUNKS,)),
            dma((CHUNKS,)),
            dma((CHUNKS, 3)),
            dma((CHUNKS, 3)),
            dma((CHUNKS, 8)),
            dma((CHUNKS, 8)),
            dma((CHUNKS, 8, 6)),
            dma((CHUNKS, 8)),
        ],
        compiler_params=pltpu.CompilerParams(
            collective_id=0, has_side_effects=True, vmem_limit_bytes=44 * 2**20
        ),
        cost_estimate=pl.CostEstimate(flops=7 * 10**9, bytes_accessed=24 * 10**6, transcendentals=0),
    )(solved, factor_rows, diag_inverse, features, covariance)


def solution(mesh):
    placed = (P("col", "row"), P(None, "col"), P(), P("row", None), P("row", "col"))
    return jax.shard_map(
        body, mesh=mesh, in_specs=placed, out_specs=P("row", "col"), check_vma=False
    )
```

```python
import jax
import jax.numpy as jnp
from jax import lax
from jax.experimental import pallas as pl
from jax.experimental.pallas import tpu as pltpu
from jax.sharding import PartitionSpec as P

F32 = jnp.float32
BF16 = jnp.bfloat16
CHUNKS = 4
KB = 256
NT = (((1,), (1,)), ((), ()))
MESH = pl.DeviceIdType.MESH

(
    PART_SIBLING, PART_OWN, REDUCE, PANEL, FROM_PREV, FROM_NEXT, FROM_OPPOSITE, ROW_DONE,
) = range(8)
SOURCE, PASS, USE, DRAIN, OTHERS, NOTHING = 8, 12, 20, 28, 30, 31
MASKS = (
    (1597889, 137, 1847426, 2097155, 1348417, 529026, 2937731, 2920458),
    (1597440, 2400655, 1048576, 2642507, 1597826, 1876615, 8258, 3191241),
    (136, 16643, 524608, 24577, 1048640, 1310784, 2359300, 786560),
    (262656, 2359360, 0, 2097160, 8192, 1573376, 2404480, 4096),
    (589, 295040, 2113540, 40968, 2413069, 778, 20493, 1310729),
    (2097156, 2359553, 16385, 2134849, 24578, 278540, 21314, 21257),
    (33283, 4, 2363392, 384, 4675, 1048577, 385, 1057024),
    (32899, 33025, 2629632, 32896, 2101321, 1048579, 4104, 262273),
    (58117, 2105856, 33418, 2101248, 2379777, 128, 3149828, 512),
    (1573120, 1368960, 132, 2654540, 524288, 2122496, 787264, 33541),
    (1572992, 802880, 1048578, 540932, 8, 1069120, 0, 16386),
    (45121, 4160, 8322, 524608, 65, 8197, 32768, 0),
    (532740, 10, 2646414, 32776, 2097280, 41472, 2621448, 2097728),
    (1589252, 2121864, 553413, 3670532, 1573504, 1089670, 16384, 541316),
    (1048576, 1052674, 2118081, 1613824, 524288, 528384, 524289, 2646021),
    (266240, 278528, 1, 513, 33289, 4224, 2097802, 16384),
)
STEPS = (
    (134254752, 205004962, 17862403, 85499683, 100926603, 140823050, 90533704, 50713750, 54826267, 219732660, 156391934, 103671222, 177134776, 182086379, 244709482, 249392337, 253143415, 259845200, 257727794, 192203921, 60710513, 65535580, 65523615, 65523615, 65523615, 65523615),
    (134254752, 205004962, 17862403, 85499683, 50496651, 198320527, 48941709, 57052329, 30301226, 265957782, 116122953, 185523531, 188406316, 223802586, 255732429, 183762426, 26556108, 249281172, 245045933, 181639982, 127782511, 65535580, 65523615, 65523615, 65523615, 65523615),
    (134254752, 205004962, 74485507, 140783934, 265865438, 31869959, 105506839, 42174010, 100017046, 174921271, 241600859, 255622631, 119888013, 183757517, 118234547, 251390540, 249273005, 114015602, 245050577, 247163726, 253496723, 126299474, 65535580, 65523615, 65523615, 65523615),
    (134254752, 205004962, 74485507, 198242622, 16757136, 35980824, 109777817, 124570253, 102065863, 164534584, 100398038, 175864759, 39566043, 248915994, 48495728, 166615249, 46381527, 41729497, 95632667, 190097973, 255613742, 126302828, 65535580, 65523615, 65523615, 65523615),
    (134254752, 205004962, 74485507, 10694974, 197239172, 77923213, 101059216, 80284131, 99024716, 97325996, 143530934, 227812165, 149841585, 210545364, 122925925, 217442262, 233015512, 236784790, 54836343, 48495470, 190093997, 259849457, 187981235, 247168370, 127330716, 65535580),
    (134254752, 205004962, 74485507, 10760510, 13681200, 16222604, 57021076, 80291939, 118085886, 52714674, 122774340, 109787212, 185920071, 215577134, 237227282, 114947607, 124579314, 181648500, 247168377, 116125010, 249273005, 179522189, 259845071, 251391185, 59082556, 65535580),
    (134254752, 205004962, 74485507, 8483134, 75607875, 50451088, 81757795, 82928148, 104425542, 150581817, 159795416, 56947668, 174954287, 33320375, 257735831, 226721267, 244688661, 106260205, 108313274, 118238523, 252033038, 166411247, 112957108, 55855447, 126303065, 65535580),
    (134254752, 205004962, 74485507, 8483134, 25276227, 42062500, 27901795, 51448464, 118232005, 36909766, 210622361, 109785927, 227944532, 244964529, 122464973, 181635854, 183761903, 174937838, 98416731, 48494774, 241600819, 259947579, 247168370, 187977107, 126299474, 65535580),
    (134254752, 205004962, 74485507, 8483134, 25276227, 78187015, 265865260, 44258072, 82578319, 118579764, 30510225, 99010966, 159685604, 149648229, 97852058, 245046119, 181640627, 251387186, 187984847, 253504850, 232062193, 248966224, 256792818, 230619548, 127231733, 65535580),
    (134254752, 205004962, 74485507, 8483134, 33664835, 78187527, 265865392, 40178444, 38391193, 118579738, 28412815, 120350741, 124901860, 123312485, 46379992, 173812945, 93027418, 255613620, 244771308, 163355438, 257272526, 230419407, 160168949, 241642039, 127776635, 65535580),
    (134254752, 205004962, 74485507, 8483134, 14790467, 265867813, 101058598, 36577959, 26288921, 58296851, 38924901, 27641754, 184906704, 122461361, 30207185, 125576726, 95856980, 116128821, 191703468, 114015731, 257849586, 251394668, 181647004, 162916341, 127773422, 65535580),
    (134254752, 205004962, 74485507, 8483134, 14790467, 26792485, 92607358, 147937831, 33900228, 211399320, 36822064, 159745817, 56947668, 111889682, 114002831, 124578896, 120355436, 251390669, 181640498, 173402012, 100513626, 246282477, 192686585, 187988344, 127860083, 65535580),
    (134254752, 205004962, 74485507, 10563902, 14131628, 48351120, 44257956, 207820824, 29985406, 109696918, 111895236, 97623095, 211383862, 214885299, 216451567, 229948404, 246852172, 255622256, 104049873, 106179385, 185951930, 183762419, 54937873, 249277907, 126303602, 65535580),
    (134254752, 205004962, 74485507, 8663358, 198236165, 50448518, 53154468, 33082642, 168153982, 82627213, 26026692, 47286036, 56944824, 211071675, 95841351, 189622758, 255457499, 115120302, 122469689, 183757517, 116128880, 259844684, 226966382, 127121396, 247167958, 65535580),
    (134254752, 205004962, 74485507, 10563902, 33664835, 78187527, 81768880, 145822636, 117868852, 210094022, 185725648, 37329330, 42147097, 216976787, 116116238, 192207533, 114015731, 257735276, 251395313, 28601295, 182200085, 160742489, 247164244, 249273521, 126298829, 65535580),
    (134254752, 205004962, 74485507, 10563902, 14790467, 34280100, 80101219, 145824295, 26319920, 116126228, 28943333, 216266261, 124582423, 251382929, 56985998, 173222734, 190126765, 245806738, 185440080, 104638961, 192309433, 232680141, 256809334, 259930608, 127264668, 65535580),
)


def pick(table, role):
    value = jnp.asarray(table[0], jnp.int32)
    for index in range(1, len(table)):
        value = jnp.where(role == index, jnp.asarray(table[index], jnp.int32), value)
    return value


def kernel(
    solved, factor, dinv, features, covariance, acc,
    sv, fv, dv, fe, res, own, sib_out, sib_in, red_out, red_in, panels,
    load_sem, sv_sem, sib_s, sib_r, red_s, red_r, gat_s, gat_r, tree_s, tree_r,
):
    row = lax.axis_index("row")
    col = lax.axis_index("col")
    y, z = row // 4, row % 4
    x, core = col // 2, col % 2

    def at(xx, yy, zz, cc):
        return {"row": ((yy + 4) % 4) * 4 + (zz + 4) % 4, "col": ((xx + 4) % 4) * 2 + cc}

    sibling = at(x, y, z, 1 - core)
    along = (at(x + 1, y, z, core), at(x - 1, y, z, core), at(x + 2, y, z, core))
    around = (
        at(x, y + 1, z, core), at(x, y - 1, z, core), at(x, y, z + 1, core), at(x, y, z - 1, core),
        at(x, y + 2, z, core), at(x, y, z + 2, core),
    )

    ahead = (y - x + 4) % 4
    role = ahead * 4 + (z - 2 * core + 4) % 4
    masks = [pick([line[index] for line in MASKS], role) for index in range(2 * CHUNKS)]

    def remote(src, dst, send, recv, device):
        return pltpu.make_async_remote_copy(
            src_ref=src, dst_ref=dst, send_sem=send, recv_sem=recv, device_id=device, device_id_type=MESH
        )

    def frames_of(place):
        chip = (x + place % 4) % 4
        half = core if place < 4 else 1 - core
        return pl.multiple_of(chip * 256 + half * 128, 128)

    def sv_load(place):
        return pltpu.make_async_copy(
            solved.at[:, pl.ds(frames_of(place), 128)], sv.at[:, pl.ds(place * 128, 128)], sv_sem.at[place]
        )

    fv_load = pltpu.make_async_copy(factor.at[pl.ds(0, KB)], fv.at[pl.ds(0, KB)], load_sem.at[0])
    fv_rest = pltpu.make_async_copy(factor.at[pl.ds(KB, 3 * KB)], fv.at[pl.ds(KB, 3 * KB)], load_sem.at[1])
    fe_load = pltpu.make_async_copy(features.at[pl.ds(frames_of(0), 128)], fe, load_sem.at[2])
    dv_load = pltpu.make_async_copy(dinv, dv, load_sem.at[3])
    acc_load = pltpu.make_async_copy(covariance, acc, load_sem.at[4])

    fv_load.start()
    for place in (4, 5, 6, 7, 0, 1, 2, 3):
        sv_load(place).start()
    fv_rest.start()
    fe_load.start()

    barrier = pltpu.get_barrier_semaphore()
    for device in (sibling,) + along + around:
        pl.semaphore_signal(barrier, inc=1, device_id=device, device_id_type=MESH)

    def rows_of(k):
        return pl.ds(pl.multiple_of(k * KB, KB), KB)

    def sib_copy(k):
        return remote(sib_out.at[k], sib_in.at[k], sib_s.at[k], sib_r.at[k], sibling)

    def red_copy(k, m):
        return remote(red_out.at[k, m], red_in.at[k, m], red_s.at[k, m], red_r.at[k, m], along[m])

    def part_sibling(k, ready=lambda: None):
        sib_out[k] = jnp.dot(fv[rows_of(k), :], sv[:, 512:], preferred_element_type=F32).astype(BF16)
        ready()
        sib_copy(k).start()

    def part_own(k):
        own[k] = jnp.dot(fv[rows_of(k), :], sv[:, :512], preferred_element_type=F32)

    def reduce(k):
        sib_copy(k).wait_recv()
        for m, first in ((2, 256), (0, 128), (1, 384)):
            piece_cols = pl.ds(first, 128)
            red_out[k, m] = (own[k, :, piece_cols] + sib_in[k, :, piece_cols].astype(F32)).astype(BF16)
            red_copy(k, m).start()
        own[k, :, :128] = own[k, :, :128] + sib_in[k, :, :128].astype(F32)

    def piece(k, chip, half):
        return panels.at[k, 8 + (chip + 4) % 4, pl.ds(pl.multiple_of(half * 128, 128), 128)]

    def gather_copy(k, m):
        chip = (x, x, x, None, x, x - 1, x + 1, x + 2)[m]
        ref = piece(k, chip, core)
        return remote(ref, ref, gat_s.at[k, m], gat_r.at[k, m], along[m] if m < 3 else sibling)

    def first_copy(k):
        ref = piece(k, x, core)
        slot = jnp.where(ahead == 1, 0, jnp.where(ahead == 3, 1, 2)) + jnp.where(core == z // 2, 0, 5)
        return remote(ref, ref, gat_s.at[k, 3], gat_r.at[k, slot], at(y, y, z, z // 2))

    def whole_copy(k, m):
        ref = panels.at[k, 8 + (x + (3, 1, 2)[m]) % 4]
        return remote(ref, ref, gat_s.at[k, m + 5], gat_r.at[k, m + 5], sibling)

    def others(k, do):
        for m, steps in enumerate((1, 3, 2)):
            @pl.when(ahead != steps)
            def _():
                do(gather_copy(k, m))

    def make_panel(k):
        @pl.when(k == 0)
        def _():
            fe_load.wait()
            dv_load.wait()
            acc_load.wait()

        for m in range(3):
            red_copy(k, m).wait_recv()
        summed = own[k, :, :128] + red_in[k, 0].astype(F32) + red_in[k, 1].astype(F32) + red_in[k, 2].astype(F32)
        cols = pl.ds(pl.multiple_of(k * KB, KB), KB)
        res[:, cols] = (fe[:, cols].astype(F32) - summed.T).astype(BF16)
        panel = lax.dot_general(res[...], dv[rows_of(k), :], NT, preferred_element_type=F32)
        panels[k, 8 + x, pl.ds(pl.multiple_of(core * 128, 128), 128)] = panel.astype(BF16)
        @pl.when(ahead != 0)
        def _():
            first_copy(k).start()

        gather_copy(k, 4).start()

    def from_along(m):
        def stage(k):
            gather_copy(k, m).wait_recv()
            gather_copy(k, m + 5).start()
        return stage

    def row_done(k):
        gather_copy(k, 4).wait_recv()

        @pl.when(ahead != 0)
        def _():
            for m in range(3):
                gather_copy(k, m + 5).wait_recv()

        @pl.when(ahead == 0)
        def _():
            for m in range(3):
                whole_copy(k, m).wait_recv()

    def tree_copy(k, u, d, src):
        return remote(panels.at[k, src], panels.at[k, u], tree_s.at[k, u, d], tree_r.at[k, u], around[d])

    def place_of(u):
        return jnp.where(u // 4 == role, 8 + (x + u % 4) % 4, u)

    def each_way(k, u, do):
        bits = lax.shift_right_logical(pick(masks, 2 * k + u // 4), (u % 4) * 6) & 63
        for d in range(6):
            @pl.when((lax.shift_right_logical(bits, d) & 1) == 1)
            def _():
                do(d)

    def hand_on(k, u):
        each_way(k, u, lambda d: tree_copy(k, u, d, place_of(u)).start())

    def drain(k):
        @pl.loop(0, 8)
        def _(u):
            each_way(k, u, lambda d: tree_copy(k, u, d, u).wait_send())

        sib_copy(k).wait_send()
        for m in range(3):
            red_copy(k, m).wait_send()
        gather_copy(k, 4).wait_send()
        others(k, lambda copy: copy.wait_send())

        @pl.when(ahead != 0)
        def _():
            first_copy(k).wait_send()
            for m in range(3):
                gather_copy(k, m + 5).wait_send()

        @pl.when(role < 2)
        def _():
            for m in range(3):
                whole_copy(k, m).wait_send()

    def use(k, u):
        first = pl.multiple_of((u // 4) * 1024 + ((x + u % 4) % 4) * 256, 256)
        rows = panels[k, 8:12].reshape(1024, KB)
        acc[:, pl.ds(first, 256)] += lax.dot_general(
            rows, panels[k, place_of(u)], NT, preferred_element_type=F32
        )

    words = tuple(pick([line[index] for line in STEPS], role) for index in range(len(STEPS[0])))
    res[...] = jnp.zeros_like(res)
    fv_load.wait()
    for place in (4, 5, 6, 7):
        sv_load(place).wait()
    for place in (0, 1, 2, 3):
        sv_load(place).wait()
    part_own(0)
    part_sibling(0, lambda: pl.semaphore_wait(barrier, 10))
    fv_rest.wait()
    dv_load.start()
    acc_load.start()

    stages = (
        part_sibling, part_own, reduce, make_panel, from_along(0), from_along(1), from_along(2), row_done,
    )

    def step(place, word):
        code = lax.shift_right_logical(word, 7 * place) & 127
        k, kind = code // 32, code % 32

        @pl.when(jnp.logical_and(kind >= USE, kind < DRAIN))
        def _():
            use(k, kind - USE)

        @pl.when(jnp.logical_and(kind >= PASS, kind < USE))
        def _():
            tree_copy(k, kind - PASS, 0, kind - PASS).wait_recv()
            hand_on(k, kind - PASS)

        @pl.when(kind < PASS)
        def _():
            for index, stage in enumerate(stages):
                @pl.when(kind == index)
                def _():
                    stage(k)

            @pl.when(kind == SOURCE)
            def _():
                gather_copy(k, 4).wait_recv()
                hand_on(k, role * 4)

            for j, m in ((1, 1), (2, 2), (3, 0)):
                @pl.when(kind == SOURCE + j)
                def _():
                    gather_copy(k, m).wait_recv()
                    gather_copy(k, m + 5).wait_recv()
                    hand_on(k, role * 4 + j)
                    whole_copy(k, m).start()

        @pl.when(kind == DRAIN)
        def _():
            drain(k)

        @pl.when(kind == OTHERS)
        def _():
            others(k, lambda copy: copy.start())

        return word

    def four_steps(_, line):
        lax.fori_loop(0, 4, step, line[0])
        return line[1:] + line[:1]

    lax.fori_loop(0, len(words), four_steps, words)


def body(solved, factor_rows, diag_inverse, features, covariance):
    any_place = pl.BlockSpec(memory_space=pl.ANY)
    dma = pltpu.SemaphoreType.DMA
    return pl.pallas_call(
        kernel,
        out_shape=pltpu.VMEM((1024, 2048), F32),
        in_specs=[any_place] * 5,
        out_specs=pl.BlockSpec(memory_space=pltpu.VMEM),
        scratch_shapes=[
            pltpu.VMEM((1024, 1024), BF16),
            pltpu.VMEM((1024, 1024), BF16),
            pltpu.VMEM((1024, 1024), BF16),
            pltpu.VMEM((128, 1024), BF16),
            pltpu.VMEM((128, 1024), BF16),
            pltpu.VMEM((CHUNKS, KB, 512), F32),
            pltpu.VMEM((CHUNKS, KB, 512), BF16),
            pltpu.VMEM((CHUNKS, KB, 512), BF16),
            pltpu.VMEM((CHUNKS, 3, KB, 128), BF16),
            pltpu.VMEM((CHUNKS, 3, KB, 128), BF16),
            pltpu.VMEM((CHUNKS, 12, 256, KB), BF16),
            dma((5,)),
            dma((8,)),
            dma((CHUNKS,)),
            dma((CHUNKS,)),
            dma((CHUNKS, 3)),
            dma((CHUNKS, 3)),
            dma((CHUNKS, 8)),
            dma((CHUNKS, 8)),
            dma((CHUNKS, 8, 6)),
            dma((CHUNKS, 8)),
        ],
        compiler_params=pltpu.CompilerParams(
            collective_id=0, has_side_effects=True, vmem_limit_bytes=44 * 2**20
        ),
        cost_estimate=pl.CostEstimate(flops=7 * 10**9, bytes_accessed=24 * 10**6, transcendentals=0),
    )(solved, factor_rows, diag_inverse, features, covariance)


def solution(mesh):
    placed = (P("col", "row"), P(None, "col"), P(), P("row", None), P("row", "col"))
    return jax.shard_map(
        body, mesh=mesh, in_specs=placed, out_specs=P("row", "col"), check_vma=False
    )
```
